32 devices in a mesh: dp: 8 (over y, x, core), tensor: 4 (over z).
Axes of the slice: x: 2, y: 2, z: 4, core: 2. Of those that a mesh axis runs over, the one named last changes fastest.
Arguments:
- inner_x: bfloat16 [2048, 8192], P(('dp', 'tensor')), parts along dimension 0, may hold values from -6 to 6
- inner_bc: bfloat16 [2048, 2048], P(('dp', 'tensor')), parts along dimension 0, may hold values from -6 to 6
- step_raw: bfloat16 [2048, 128], P(('dp', 'tensor')), parts along dimension 0, may hold values from -5 to 5
- conv_state_x: bfloat16 [24, 8192], P('dp', 'tensor'), parts along dimension 0, may hold values from -6 to 6
- conv_state_bc: bfloat16 [24, 2048], P('dp'), parts along dimension 0, may hold values from -6 to 6
- conv_weight_x: bfloat16 [4, 8192], P(None, 'tensor'), may hold values from -3 to 3
- conv_bias_x: bfloat16 [8192], P('tensor'), may hold values from -3 to 3
- conv_weight_bc: bfloat16 [4, 2048], replicated, may hold values from -3 to 3
- conv_bias_bc: bfloat16 [2048], replicated, may hold values from -3 to 3
- step_bias: float32 [128], P('tensor'), may hold values from -4 to -2
- decay_rate: float32 [128], P('tensor'), may hold values from 0 to 1, as said below
- skip_gain: float32 [128], P('tensor'), may hold values from 0.5 to 1.5
- norm_weight: bfloat16 [8192], replicated, may hold values from 0.5 to 1.5
- scan_state: float32 [1024, 64, 256], P(('dp', 'tensor')), parts along dimension 0, may hold values from -3 to 3
Outputs:
- normed: bfloat16 [2048, 8192], P(('dp', 'tensor')), parts along dimension 0
- final_state: float32 [1024, 64, 256], P(('dp', 'tensor')), parts along dimension 0
- conv_tail_x: bfloat16 [24, 8192], P('dp', 'tensor'), parts along dimension 0
- conv_tail_bc: bfloat16 [24, 2048], P('dp', 'tensor'), parts along dimension 0
The draws below stay inside these ranges and needn't reach their ends.
There are 8 independent parts, one for each index of `dp`. The reference program is written for one: setup_inputs(seed, part) draws one part's arguments, and reference() takes and returns one part's arrays. A program takes and returns all parts, laid end to end along the dimension named above; an argument that names none is the same for every part. Nothing has to cross between parts.
Inputs may be any that keep to these rules, and one draw needn't show every extreme that they name: decay_rate lies between 2 / 256 and 1 / 2.
All inputs are finite; a program needn't handle non-finite values.
Results may differ from the reference program's by a relative error of at most 0.0051.
Values may be sent and summed in bfloat16 or wider, within the bound.
A program may use at most 64 MiB of HBM per device.

```python
import math
import jax
import jax.numpy as jnp
from jax import lax

HEADS = 128
HEAD_DIM = 64
STATE = 256
GROUPS = 4
CONV_K = 4
TOKENS = 256
INNER = 8192


def draw_decay_rate(key, part):
    lower = math.log(2.0 / TOKENS)
    upper = math.log(0.5)
    unit = jax.random.uniform(key, (HEADS,), jnp.float32)
    return jnp.exp(lower + (upper - lower) * unit).astype(jnp.float32)


def block_levels(key, extent, cuts, smallest, top_value):
    level = 1.0
    for position, shards_of in cuts:
        steps = jax.random.uniform(jax.random.fold_in(jax.random.fold_in(key, 6), position), (shards_of,), jnp.float32, smallest / len(cuts), top_value / len(cuts))
        level = level * jnp.repeat(jnp.exp(steps), extent[position] // shards_of).reshape((-1,) + (1,) * (len(extent) - 1 - position))
    return level


def normal_values(key, dims, scale, reach, shards=(), kind=jnp.bfloat16):
    entries = scale * jax.random.normal(key, dims, jnp.float32)
    if shards:
        entries = entries * block_levels(key, dims, shards, -0.22, 0.18)
    return jnp.clip(entries, -reach, reach).astype(kind)


def setup_inputs(seed: int = 0, part: int = 0) -> dict:
    keys = jax.random.split(jax.random.key(seed), 15)
    part_keys = jax.random.split(jax.random.fold_in(keys[14], part), 15)
    return {
        "inner_x": normal_values(part_keys[0], (TOKENS, INNER), 1.0, 6.0, ((0, 4),)),
        "inner_bc": normal_values(part_keys[1], (TOKENS, 2 * GROUPS * STATE), 1.0, 6.0, ((0, 4),)),
        "step_raw": normal_values(part_keys[2], (TOKENS, HEADS), 1.0, 5.0, ((0, 4),)),
        "conv_state_x": normal_values(part_keys[3], (CONV_K - 1, INNER), 1.0, 6.0, ((1, 4),)),
        "conv_state_bc": normal_values(part_keys[4], (CONV_K - 1, 2 * GROUPS * STATE), 1.0, 6.0),
        "conv_weight_x": normal_values(keys[5], (CONV_K, INNER), CONV_K ** -0.5, 3.0, ((1, 4),)),
        "conv_bias_x": normal_values(keys[6], (INNER,), 0.5, 3.0, ((0, 4),)),
        "conv_weight_bc": normal_values(keys[7], (CONV_K, 2 * GROUPS * STATE), CONV_K ** -0.5, 3.0),
        "conv_bias_bc": normal_values(keys[8], (2 * GROUPS * STATE,), 0.5, 3.0),
        "step_bias": jnp.clip(-4.0 + 2.0 * jax.random.uniform(keys[9], (HEADS,), jnp.float32) ** block_levels(keys[9], (HEADS,), ((0, 4),), -0.2, 0.2), -4.0, -2.0),
        "decay_rate": draw_decay_rate(jax.random.fold_in(keys[14], 71), part),
        "skip_gain": jnp.clip(0.5 + 1.0 * jax.random.uniform(keys[11], (HEADS,), jnp.float32) ** block_levels(keys[11], (HEADS,), ((0, 4),), -0.2, 0.2), 0.5, 1.5),
        "norm_weight": jnp.clip(1.0 + 0.1 * jax.random.normal(keys[12], (INNER,), jnp.float32), 0.5, 1.5).astype(jnp.bfloat16),
        "scan_state": normal_values(part_keys[13], (HEADS, HEAD_DIM, STATE), 0.3, 3.0, ((0, 4),), jnp.float32),
    }


EPSILON = 1e-05

def causal_conv(raw, state, weight, bias):
    length = raw.shape[0]
    padded = jnp.concatenate([state.astype(jnp.float32), raw.astype(jnp.float32)], axis=0)
    total = jnp.zeros(raw.shape, jnp.float32) + bias.astype(jnp.float32)[None, :]
    for kernel_tap in range(CONV_K):
        total = total + weight[kernel_tap].astype(jnp.float32)[None, :] * padded[kernel_tap:kernel_tap + length]
    return jax.nn.silu(total).astype(jnp.bfloat16)

def state_mix(mixed_x, mixed_bc, step_raw, step_bias, decay_rate, skip_gain, scan_state, groups_here):
    length = mixed_x.shape[0]
    heads_here = step_raw.shape[1]
    per_group = heads_here // groups_here
    step_size = jax.nn.softplus(step_raw.astype(jnp.float32) + step_bias[None, :])
    running = jnp.cumsum(-step_size * decay_rate[None, :], axis=0)
    halves = mixed_bc.reshape(length, groups_here, 2, STATE)
    input_map = halves[:, :, 0, :]
    output_map = halves[:, :, 1, :]
    step_cols = jnp.transpose(step_size)
    running_cols = jnp.transpose(running)
    query_rows = min(512, length)
    pieces = []
    for row_start in range(0, length, query_rows):
        row_stop = row_start + query_rows
        scores = jnp.einsum('tgn,sgn->gts', output_map[row_start:row_stop].astype(jnp.float32), input_map[:row_stop].astype(jnp.float32), precision=lax.Precision.HIGHEST)
        causal = row_start + lax.broadcasted_iota(jnp.int32, (query_rows, row_stop), 0) >= lax.broadcasted_iota(jnp.int32, (query_rows, row_stop), 1)
        visible = mixed_x[:row_stop]

        def one_head(item, scores=scores, causal=causal, visible=visible, row_start=row_start, row_stop=row_stop):
            head_index, step_head, running_head = item
            group_scores = lax.dynamic_index_in_dim(scores, head_index // per_group, 0, keepdims=False)
            log_gap = running_head[row_start:row_stop, None] - running_head[None, :row_stop]
            decayed = jnp.exp(jnp.where(causal, log_gap, 0.0))
            weights = jnp.where(causal, group_scores * decayed * step_head[None, :row_stop], 0.0).astype(jnp.bfloat16)
            values = lax.dynamic_slice_in_dim(visible, head_index * HEAD_DIM, HEAD_DIM, 1)
            return jnp.dot(weights, values, preferred_element_type=jnp.float32)
        local_mix = lax.map(one_head, (jnp.arange(heads_here, dtype=jnp.int32), step_cols, running_cols))
        pieces.append(jnp.transpose(local_mix, (1, 0, 2)).reshape(query_rows, heads_here * HEAD_DIM))
    local_all = jnp.concatenate(pieces, axis=0)
    grouped_state = scan_state.reshape(groups_here, per_group, HEAD_DIM, STATE)
    carried = jnp.einsum('tgn,ghpn->tghp', output_map.astype(jnp.float32), grouped_state, precision=lax.Precision.HIGHEST)
    carried = carried.reshape(length, heads_here, HEAD_DIM) * jnp.exp(running)[:, :, None]
    channels = mixed_x.reshape(length, heads_here, HEAD_DIM).astype(jnp.float32)
    mixed = local_all.reshape(length, heads_here, HEAD_DIM) + carried + skip_gain[None, :, None] * channels
    mixed_y = mixed.reshape(length, heads_here * HEAD_DIM).astype(jnp.bfloat16)
    tail_decay = jnp.exp(running[length - 1][None, :] - running) * step_size
    weighted = (input_map.astype(jnp.float32)[:, :, None, :] * tail_decay.reshape(length, groups_here, per_group)[:, :, :, None]).astype(jnp.bfloat16)
    gathered_in = jnp.einsum('tghp,tghn->ghpn', mixed_x.reshape(length, groups_here, per_group, HEAD_DIM).astype(jnp.float32), weighted.astype(jnp.float32), precision=lax.Precision.HIGHEST)
    final = jnp.exp(running[length - 1]).reshape(groups_here, per_group)[:, :, None, None] * grouped_state + gathered_in
    return (mixed_y, final.reshape(heads_here, HEAD_DIM, STATE))

def group_norm(mixed_y, norm_weight):
    rows = mixed_y.shape[0]
    values = mixed_y.astype(jnp.float32).reshape(rows, GROUPS, INNER // GROUPS)
    mean_square = lax.optimization_barrier(jnp.mean(values * values, axis=2, keepdims=True))
    scaled = (values * lax.rsqrt(mean_square + EPSILON)).reshape(rows, INNER)
    return (scaled * norm_weight.astype(jnp.float32)[None, :]).astype(jnp.bfloat16)

def reference(inner_x, inner_bc, step_raw, conv_state_x, conv_state_bc, conv_weight_x, conv_bias_x, conv_weight_bc, conv_bias_bc, step_bias, decay_rate, skip_gain, norm_weight, scan_state):
    mixed_x = causal_conv(inner_x, conv_state_x, conv_weight_x, conv_bias_x)
    mixed_bc = causal_conv(inner_bc, conv_state_bc, conv_weight_bc, conv_bias_bc)
    mixed_y, final_state = state_mix(mixed_x, mixed_bc, step_raw, step_bias, decay_rate, skip_gain, scan_state, GROUPS)
    normed = group_norm(mixed_y, norm_weight)
    return (normed, final_state, inner_x[TOKENS - CONV_K + 1:], inner_bc[TOKENS - CONV_K + 1:])
```

```python
import functools
import math

import jax
import jax.numpy as jnp
from jax import lax
from jax.experimental import pallas as pl
from jax.experimental.pallas import tpu as pltpu
from jax.sharding import PartitionSpec as P

HEAD_DIM = 64
STATE = 256
GROUPS = 4
CONV_K = 4
EPSILON = 1e-05
LOG2E = math.log2(math.e)
CHUNK = 512
PAIR = 2 * HEAD_DIM
BLOCK = 256
MESH = pl.DeviceIdType.MESH
F32 = jnp.float32
BF16 = jnp.bfloat16
HIGHEST = lax.Precision.HIGHEST


def dot_nt(a, b, precision=None):
    return lax.dot_general(
        a, b, (((1,), (1,)), ((), ())), precision=precision, preferred_element_type=F32
    )


def dot_tn(a, b):
    return lax.dot_general(a, b, (((0,), (0,)), ((), ())), preferred_element_type=F32)


def silu(total):
    half = 0.5 * total
    return half + half * jnp.tanh(half)


def column_of(row):
    width = row.shape[1]
    eye = lax.broadcasted_iota(jnp.int32, (width, width), 0) == lax.broadcasted_iota(
        jnp.int32, (width, width), 1
    )
    return jnp.sum(jnp.where(eye, jnp.broadcast_to(row, (width, width)), 0.0), axis=1, keepdims=True)


def kernel(
    n,
    chunk,
    x_ref,
    bc_ref,
    step_ref,
    state_x_ref,
    state_bc_ref,
    weight_x_ref,
    bias_x_ref,
    weight_bc_ref,
    bias_bc_ref,
    step_bias_ref,
    decay_ref,
    skip_ref,
    norm_ref,
    scan_ref,
    normed_ref,
    final_ref,
    tail_x_ref,
    tail_bc_ref,
    xg,
    bcg,
    stg,
    ysend,
    yrecv,
    scan,
    fout,
    nout,
    conv_rows,
    maps,
    masked_scores,
    run_cols,
    gap_cols,
    gap_rows,
    skip_lanes,
    small_send,
    small_recv,
    x_send,
    x_recv,
    y_send,
    y_recv,
    scan_sem,
    fout_sem,
    nout_sem,
):
    me = lax.axis_index("tensor")
    rows = x_ref.shape[0]
    length = n * rows
    width = xg.shape[1]
    chunks = width // chunk
    chunk_heads = chunk // HEAD_DIM
    heads = width // HEAD_DIM
    group_width = 2 * STATE
    blocks = length // BLOCK
    group = me * GROUPS // n

    def ahead(i):
        return lax.rem(me + i, n)

    def behind(i):
        return lax.rem(me + n - i, n)

    def row_span(device):
        return pl.ds(pl.multiple_of(device * rows, rows), rows)

    def chunk_span(base, k):
        return pl.ds(pl.multiple_of(base + k * chunk, chunk), chunk)

    def group_span(device):
        start = (device * GROUPS // n) * group_width
        return pl.ds(pl.multiple_of(start, group_width), group_width)

    def bc_copy(i, peer, source):
        src, dst = bc_ref.at[:, group_span(peer)], bcg.at[row_span(source), :]
        if i == 0:
            return pltpu.make_async_copy(src, dst, small_recv.at[0, 0])
        return pltpu.make_async_remote_copy(
            src, dst, small_send.at[0, i], small_recv.at[0, i], {"tensor": peer}, MESH
        )

    def step_copy(i, peer, source):
        src, dst = step_ref, stg.at[row_span(source), :]
        if i == 0:
            return pltpu.make_async_copy(src, dst, small_recv.at[1, 0])
        return pltpu.make_async_remote_copy(
            src, dst, small_send.at[1, i], small_recv.at[1, i], {"tensor": peer}, MESH
        )

    def x_copy(i, k, peer, source):
        src = x_ref.at[:, chunk_span(peer * width, k)]
        dst = xg.at[row_span(source), chunk_span(0, k)]
        if i == 0:
            return pltpu.make_async_copy(src, dst, x_recv.at[0, k])
        return pltpu.make_async_remote_copy(
            src, dst, x_send.at[i, k], x_recv.at[i, k], {"tensor": peer}, MESH
        )

    def y_copy(i, k, peer, source):
        src = ysend.at[row_span(peer), chunk_span(0, k)]
        dst = yrecv.at[:, chunk_span(source * width, k)]
        if i == 0:
            return pltpu.make_async_copy(src, dst, y_recv.at[0, k])
        return pltpu.make_async_remote_copy(
            src, dst, y_send.at[i, k], y_recv.at[i, k], {"tensor": peer}, MESH
        )

    def scan_copy(k):
        return pltpu.make_async_copy(
            scan_ref.at[chunk_span(0, k), :], scan.at[chunk_span(0, k), :], scan_sem.at[k]
        )

    def fout_copy(k):
        return pltpu.make_async_copy(
            fout.at[chunk_span(0, k), :], final_ref.at[chunk_span(0, k), :], fout_sem.at[k]
        )

    def start_to_all(copy):
        for i in range(n):
            copy(i, ahead(i), me).start()

    def arrive_from_all(copy):
        for i in range(n):
            if i == 0:
                copy(0, me, me).wait()
            else:
                copy(i, ahead(i), behind(i)).wait_recv()

    barrier = pltpu.get_barrier_semaphore()
    for i in range(1, n):
        pl.semaphore_signal(barrier, inc=1, device_id={"tensor": ahead(i)}, device_id_type=MESH)
    pl.semaphore_wait(barrier, n - 1)

    start_to_all(step_copy)
    start_to_all(bc_copy)
    for k in range(chunks):
        start_to_all(lambda i, peer, source: x_copy(i, k, peer, source))
    for k in range(chunks):
        scan_copy(k).start()

    arrive_from_all(step_copy)
    lanes_all = stg.shape[1]
    pick = (
        lax.broadcasted_iota(jnp.int32, (heads, lanes_all), 1)
        == lax.broadcasted_iota(jnp.int32, (heads, lanes_all), 0) + me * heads
    ).astype(BF16)
    bias_row, decay_row = step_bias_ref[...], decay_ref[...]
    bias_col, decay_col = column_of(bias_row), column_of(decay_row)
    below = (
        lax.broadcasted_iota(jnp.int32, (BLOCK, BLOCK), 0)
        >= lax.broadcasted_iota(jnp.int32, (BLOCK, BLOCK), 1)
    )
    lower = below.astype(F32)
    base_cols = jnp.zeros((1, heads), F32)
    base_rows = jnp.zeros((heads, 1), F32)
    for b in range(blocks):
        span = slice(b * BLOCK, (b + 1) * BLOCK)
        raw = stg[span, :]
        step = jnp.log1p(jnp.exp(dot_nt(raw, pick) + bias_row))
        run = base_cols - jnp.dot(
            lower, step * decay_row, precision=HIGHEST, preferred_element_type=F32
        )
        base_cols = run[BLOCK - 1 :, :]
        gap = run * LOG2E - jnp.log(step) * LOG2E
        for k in range(chunks):
            run_cols[k, span, :] = run[:, k * chunk_heads : (k + 1) * chunk_heads] * LOG2E
            gap_cols[k, span, :] = gap[:, k * chunk_heads : (k + 1) * chunk_heads]
        step = jnp.log1p(jnp.exp(dot_nt(pick, raw) + bias_col))
        run = base_rows - dot_nt(step * decay_col, lower, precision=HIGHEST)
        base_rows = run[:, BLOCK - 1 :]
        gap = run * LOG2E - jnp.log(step) * LOG2E
        for k in range(chunks):
            gap_rows[k, :, span] = gap[k * chunk_heads : (k + 1) * chunk_heads, :]
    spread = (
        lax.broadcasted_iota(jnp.int32, (heads, width), 1) // HEAD_DIM
        == lax.broadcasted_iota(jnp.int32, (heads, width), 0)
    ).astype(F32)
    skip_lanes[...] = jnp.dot(
        jnp.broadcast_to(skip_ref[...], (8, heads)),
        spread,
        precision=HIGHEST,
        preferred_element_type=F32,
    )

    def convolve(raw, state, weight, bias):
        conv_rows[8 - CONV_K + 1 : 8, :] = state.astype(F32)
        conv_rows[8:, :] = raw.astype(F32)
        total = jnp.broadcast_to(bias.astype(F32), (length, PAIR))
        for tap in range(CONV_K):
            start = 8 - CONV_K + 1 + tap
            total = total + weight[tap : tap + 1, :].astype(F32) * conv_rows[start : start + length, :]
        return silu(total).astype(BF16)

    arrive_from_all(bc_copy)
    for j in range(group_width // PAIR):
        cols = pl.ds(pl.multiple_of(group * group_width + j * PAIR, PAIR), PAIR)
        maps[:, j * PAIR : (j + 1) * PAIR] = convolve(
            bcg[:, j * PAIR : (j + 1) * PAIR],
            state_bc_ref[:, cols],
            weight_bc_ref[:, cols],
            bias_bc_ref[:, cols],
        )
    for q in range(blocks):
        here = slice(q * BLOCK, (q + 1) * BLOCK)
        for s in range(q + 1):
            there = slice(s * BLOCK, (s + 1) * BLOCK)
            scores = dot_nt(maps[here, STATE:], maps[there, :STATE])
            masked_scores[here, there] = jnp.where(below, scores, 0.0) if s == q else scores
    tail_cols = tail_bc_ref.shape[1]
    offset = pl.multiple_of(me * tail_cols - group * group_width, tail_cols)
    tail_bc_ref[...] = bcg[length - 16 :, pl.ds(offset, tail_cols)][16 - CONV_K + 1 :, :]

    first_lanes = lax.broadcasted_iota(jnp.int32, (BLOCK, PAIR), 1) < HEAD_DIM
    first_rows = lax.broadcasted_iota(jnp.int32, (PAIR, 1), 0) < HEAD_DIM

    def one_chunk(k, carry):
        arrive_from_all(lambda i, peer, source: x_copy(i, k, peer, source))
        scan_copy(k).wait()
        for j in range(chunk // PAIR):
            cols = pl.ds(pl.multiple_of(k * chunk + j * PAIR, PAIR), PAIR)
            mixed = convolve(
                xg[:, cols], state_x_ref[:, cols], weight_x_ref[:, cols], bias_x_ref[:, cols]
            )
            old = scan[cols, :]
            high = old.astype(BF16)
            low = (old - high.astype(F32)).astype(BF16)
            ends = [run_cols[k, length - 1 :, 2 * j + h : 2 * j + h + 1] for h in (0, 1)]
            gained = None
            for q in range(blocks):
                here = slice(q * BLOCK, (q + 1) * BLOCK)
                values = mixed[here, :].astype(F32)
                out = maps[here, STATE:]
                run = [
                    jnp.broadcast_to(run_cols[k, here, 2 * j + h : 2 * j + h + 1], (BLOCK, PAIR))
                    for h in (0, 1)
                ]
                total = (dot_nt(out, high) + dot_nt(out, low)) * jnp.where(
                    first_lanes, jnp.exp2(run[0]), jnp.exp2(run[1])
                )
                total = total + skip_lanes[0:1, cols] * values
                for s in range(q + 1):
                    there = slice(s * BLOCK, (s + 1) * BLOCK)
                    for h in (0, 1):
                        row = gap_rows[k, 2 * j + h : 2 * j + h + 1, there]
                        wide = jnp.concatenate([run[h]] * (BLOCK // PAIR), axis=1)
                        decayed = jnp.exp2(jnp.minimum(wide - row, 64.0))
                        weights = (masked_scores[here, there] * decayed).astype(BF16)
                        keep = first_lanes if h == 0 else jnp.logical_not(first_lanes)
                        seen = jnp.where(keep, mixed[there, :].astype(F32), 0.0).astype(BF16)
                        total = total + jnp.dot(weights, seen, preferred_element_type=F32)
                ysend[here, cols] = total.astype(BF16)
                tails = [
                    jnp.exp2(ends[h] - gap_cols[k, here, 2 * j + h : 2 * j + h + 1]) for h in (0, 1)
                ]
                tailed = (values * jnp.where(first_lanes, tails[0], tails[1])).astype(BF16)
                part = dot_tn(tailed, maps[here, :STATE])
                gained = part if gained is None else gained + part
            fade = jnp.where(first_rows, jnp.exp2(ends[0]), jnp.exp2(ends[1]))
            fout[cols, :] = fade * old + gained
        start_to_all(lambda i, peer, source: y_copy(i, k, peer, source))
        fout_copy(k).start()
        return carry

    lax.fori_loop(0, chunks, one_chunk, 0)
    tail_x_ref[...] = xg[length - 16 :, :][16 - CONV_K + 1 :, :]

    members = max(1, n // GROUPS)
    norm_width = nout.shape[1] // GROUPS

    def arrive(i):
        for k in range(chunks):
            if i == 0:
                y_copy(0, k, me, me).wait()
            else:
                y_copy(i, k, ahead(i), behind(i)).wait_recv()

    def nout_copy(q, span):
        return pltpu.make_async_copy(nout.at[:, span], normed_ref.at[:, span], nout_sem.at[q])

    if members > 1:
        for i in range(n):
            arrive(i)
    spans = []
    for q in range(GROUPS):
        if members == 1:
            arrive(q)
            start = behind(q) * norm_width
        else:
            start = q * norm_width
        span = pl.ds(pl.multiple_of(start, norm_width), norm_width)
        values = yrecv[:, span].astype(F32)
        square = jnp.mean(values * values, axis=1, keepdims=True)
        scaled = values * lax.rsqrt(square + EPSILON)
        nout[:, span] = (scaled * norm_ref[:, span].astype(F32)).astype(BF16)
        nout_copy(q, span).start()
        spans.append(span)

    for i in range(1, n):
        step_copy(i, ahead(i), me).wait_send()
        bc_copy(i, ahead(i), me).wait_send()
        for k in range(chunks):
            x_copy(i, k, ahead(i), me).wait_send()
            y_copy(i, k, ahead(i), me).wait_send()
    for k in range(chunks):
        fout_copy(k).wait()
    for q in range(GROUPS):
        nout_copy(q, spans[q]).wait()


def local(
    inner_x,
    inner_bc,
    step_raw,
    conv_state_x,
    conv_state_bc,
    conv_weight_x,
    conv_bias_x,
    conv_weight_bc,
    conv_bias_bc,
    step_bias,
    decay_rate,
    skip_gain,
    norm_weight,
    scan_state,
):
    n = lax.axis_size("tensor")
    rows, inner = inner_x.shape
    heads = step_bias.shape[0]
    width = heads * HEAD_DIM
    length = n * rows
    chunk = min(CHUNK, width)
    chunks = width // chunk
    chunk_heads = chunk // HEAD_DIM
    group_width = 2 * STATE
    tail_cols = inner_bc.shape[1] // n
    dma = pltpu.SemaphoreType.DMA
    hbm = pl.BlockSpec(memory_space=pl.ANY)
    vmem = pl.BlockSpec(memory_space=pltpu.VMEM)
    outs = pl.pallas_call(
        functools.partial(kernel, n, chunk),
        out_shape=(
            jax.ShapeDtypeStruct((rows, inner), BF16),
            jax.ShapeDtypeStruct((width, STATE), F32),
            jax.ShapeDtypeStruct((CONV_K - 1, width), BF16),
            jax.ShapeDtypeStruct((CONV_K - 1, tail_cols), BF16),
        ),
        in_specs=[hbm] * 3 + [vmem] * 10 + [hbm],
        out_specs=(hbm, hbm, vmem, vmem),
        scratch_shapes=[
            pltpu.VMEM((length, width), BF16),
            pltpu.VMEM((length, group_width), BF16),
            pltpu.VMEM((length, step_raw.shape[1]), BF16),
            pltpu.VMEM((length, width), BF16),
            pltpu.VMEM((rows, inner), BF16),
            pltpu.VMEM((width, STATE), F32),
            pltpu.VMEM((width, STATE), F32),
            pltpu.VMEM((rows, inner), BF16),
            pltpu.VMEM((length + 8, PAIR), F32),
            pltpu.VMEM((length, group_width), BF16),
            pltpu.VMEM((length, length), F32),
            pltpu.VMEM((chunks, length, chunk_heads), F32),
            pltpu.VMEM((chunks, length, chunk_heads), F32),
            pltpu.VMEM((chunks, chunk_heads, length), F32),
            pltpu.VMEM((8, width), F32),
            dma((2, n)),
            dma((2, n)),
            dma((n, chunks)),
            dma((n, chunks)),
            dma((n, chunks)),
            dma((n, chunks)),
            dma((chunks,)),
            dma((chunks,)),
            dma((GROUPS,)),
        ],
        compiler_params=pltpu.CompilerParams(
            collective_id=0, has_side_effects=True, vmem_limit_bytes=48 * 1024 * 1024
        ),
    )(
        inner_x,
        inner_bc,
        step_raw,
        conv_state_x,
        conv_state_bc,
        conv_weight_x,
        conv_bias_x.reshape(1, -1),
        conv_weight_bc,
        conv_bias_bc.reshape(1, -1),
        step_bias.reshape(1, -1),
        decay_rate.reshape(1, -1),
        skip_gain.reshape(1, -1),
        norm_weight.reshape(1, -1),
        scan_state.reshape(width, STATE),
    )
    normed, final_state, tail_x, tail_bc = outs
    return (normed, final_state.reshape(heads, HEAD_DIM, STATE), tail_x, tail_bc)


def solution(mesh):
    return jax.shard_map(
        local,
        mesh=mesh,
        in_specs=(
            P(("dp", "tensor"), None),
            P(("dp", "tensor"), None),
            P(("dp", "tensor"), None),
            P("dp", "tensor"),
            P("dp", None),
            P(None, "tensor"),
            P("tensor"),
            P(),
            P(),
            P("tensor"),
            P("tensor"),
            P("tensor"),
            P(),
            P(("dp", "tensor"), None, None),
        ),
        out_specs=(
            P(("dp", "tensor"), None),
            P(("dp", "tensor"), None, None),
            P("dp", "tensor"),
            P("dp", "tensor"),
        ),
        check_vma=False,
    )
```

```python
import functools
import math

import jax
import jax.numpy as jnp
from jax import lax
from jax.experimental import pallas as pl
from jax.experimental.pallas import tpu as pltpu
from jax.sharding import PartitionSpec as P

HEAD_DIM = 64
STATE = 256
GROUPS = 4
CONV_K = 4
EPSILON = 1e-05
LOG2E = math.log2(math.e)
CHUNK = 512
SPLITS = (4, 8, 1, 1)
VMEM_LIMIT = 60 * 1024 * 1024
PAIR = 2 * HEAD_DIM
BLOCK = 256
MESH = pl.DeviceIdType.MESH
F32 = jnp.float32
BF16 = jnp.bfloat16
HIGHEST = lax.Precision.HIGHEST


def dot_nt(a, b, precision=None):
    return lax.dot_general(
        a, b, (((1,), (1,)), ((), ())), precision=precision, preferred_element_type=F32
    )


def dot_tn(a, b):
    return lax.dot_general(a, b, (((0,), (0,)), ((), ())), preferred_element_type=F32)


def silu(total):
    half = 0.5 * total
    return half + half * jnp.tanh(half)


def column_of(row):
    width = row.shape[1]
    eye = lax.broadcasted_iota(jnp.int32, (width, width), 0) == lax.broadcasted_iota(
        jnp.int32, (width, width), 1
    )
    return jnp.sum(jnp.where(eye, jnp.broadcast_to(row, (width, width)), 0.0), axis=1, keepdims=True)


def kernel(
    n,
    chunk,
    x_ref,
    bc_ref,
    step_ref,
    *refs,
):
    small_in = refs[:10]
    scan_ref, normed_out, final_out, tail_x_out, tail_bc_out = refs[10:15]
    small = refs[15:25]
    (
        state_x_ref,
        state_bc_ref,
        weight_x_ref,
        bias_x_in,
        weight_bc_ref,
        bias_bc_in,
        step_bias_ref,
        decay_ref,
        skip_ref,
        norm_in,
    ) = small
    (
        xg,
        bcg,
        stg,
        ysend,
        yrecv,
        scan,
        fout,
        nout,
        tail_x_ref,
        tail_bc_ref,
        conv_rows,
        maps,
        masked_scores,
        run_cols,
        gap_cols,
        gap_rows,
        skip_lanes,
        bias_x_ref,
        bias_bc_ref,
        norm_ref,
        small_send,
        small_recv,
        x_send,
        x_recv,
        y_send,
        y_recv,
        scan_sem,
        local_sem,
        fout_sem,
        nout_sem,
        tail_sem,
    ) = refs[25:]
    me = lax.axis_index("tensor")
    rows = x_ref.shape[0]
    length = n * rows
    width = xg.shape[1]
    chunks = width // chunk
    chunk_heads = chunk // HEAD_DIM
    heads = width // HEAD_DIM
    group_width = 2 * STATE
    blocks = length // BLOCK
    group = me * GROUPS // n

    order = list(range(n // 2, n)) + list(range(1, n // 2)) + [0]

    def partner(i):
        other, bit = me, 1
        while bit <= i:
            if i & bit:
                other = other + bit - 2 * bit * ((me // bit) % 2)
            bit *= 2
        return other

    def row_span(device):
        return pl.ds(pl.multiple_of(device * rows, rows), rows)

    def chunk_span(base, k):
        return pl.ds(pl.multiple_of(base + k * chunk, chunk), chunk)

    def group_span(device):
        start = (device * GROUPS // n) * group_width
        return pl.ds(pl.multiple_of(start, group_width), group_width)

    def bc_copy(i, peer, source):
        src, dst = bc_ref.at[:, group_span(peer)], bcg.at[row_span(source), :]
        if i == 0:
            return pltpu.make_async_copy(src, dst, small_recv.at[0, 0])
        return pltpu.make_async_remote_copy(
            src, dst, small_send.at[0, i], small_recv.at[0, i], {"tensor": peer}, MESH
        )

    def step_copy(i, peer, source):
        src, dst = step_ref, stg.at[row_span(source), :]
        if i == 0:
            return pltpu.make_async_copy(src, dst, small_recv.at[1, 0])
        return pltpu.make_async_remote_copy(
            src, dst, small_send.at[1, i], small_recv.at[1, i], {"tensor": peer}, MESH
        )

    def x_copy(i, k, peer, source):
        src = x_ref.at[:, chunk_span(peer * width, k)]
        dst = xg.at[row_span(source), chunk_span(0, k)]
        if i == 0:
            return pltpu.make_async_copy(src, dst, x_recv.at[0, k])
        return pltpu.make_async_remote_copy(
            src, dst, x_send.at[i, k], x_recv.at[i, k], {"tensor": peer}, MESH
        )

    def y_copy(i, k, peer, source):
        src = ysend.at[row_span(peer), chunk_span(0, k)]
        dst = yrecv.at[:, chunk_span(source * width, k)]
        if i == 0:
            return pltpu.make_async_copy(src, dst, y_recv.at[0, k])
        return pltpu.make_async_remote_copy(
            src, dst, y_send.at[i, k], y_recv.at[i, k], {"tensor": peer}, MESH
        )

    def scan_copy(k):
        return pltpu.make_async_copy(
            scan_ref.at[chunk_span(0, k), :], scan.at[chunk_span(0, k), :], scan_sem.at[k]
        )

    def small_copy(i):
        return pltpu.make_async_copy(small_in[i], small[i], local_sem.at[i])

    def fout_copy(k):
        span = chunk_span(0, k)
        return pltpu.make_async_copy(fout.at[span, :], final_out.at[span, :], fout_sem.at[k])

    def nout_copy(q, span):
        return pltpu.make_async_copy(nout.at[:, span], normed_out.at[:, span], nout_sem.at[q])

    tail_copies = (
        pltpu.make_async_copy(tail_x_ref, tail_x_out, tail_sem.at[0]),
        pltpu.make_async_copy(tail_bc_ref, tail_bc_out, tail_sem.at[1]),
    )

    def start_to_all(copy):
        for i in order:
            copy(i, partner(i), me).start()

    def arrive_from_all(copy):
        for i in range(n):
            if i == 0:
                copy(0, me, me).wait()
            else:
                copy(i, partner(i), partner(i)).wait_recv()

    for i in range(len(small)):
        small_copy(i).start()
    barrier = pltpu.get_barrier_semaphore()
    for i in range(1, n):
        pl.semaphore_signal(barrier, inc=1, device_id={"tensor": partner(i)}, device_id_type=MESH)
    pl.semaphore_wait(barrier, n - 1)

    start_to_all(step_copy)
    start_to_all(bc_copy)
    for k in range(chunks):
        start_to_all(lambda i, peer, source: x_copy(i, k, peer, source))
    for k in range(chunks):
        scan_copy(k).start()

    for i in range(len(small)):
        small_copy(i).wait()
    bias_x_ref[...] = bias_x_in[...].astype(F32)
    bias_bc_ref[...] = bias_bc_in[...].astype(F32)
    norm_ref[...] = norm_in[...].astype(F32)

    arrive_from_all(step_copy)
    lanes_all = stg.shape[1]
    pick = (
        lax.broadcasted_iota(jnp.int32, (heads, lanes_all), 1)
        == lax.broadcasted_iota(jnp.int32, (heads, lanes_all), 0) + me * heads
    ).astype(BF16)
    bias_row, decay_row = step_bias_ref[...], decay_ref[...]
    bias_col, decay_col = column_of(bias_row), column_of(decay_row)
    below = (
        lax.broadcasted_iota(jnp.int32, (BLOCK, BLOCK), 0)
        >= lax.broadcasted_iota(jnp.int32, (BLOCK, BLOCK), 1)
    )
    lower = below.astype(F32)
    base_cols = jnp.zeros((1, heads), F32)
    base_rows = jnp.zeros((heads, 1), F32)
    for b in range(blocks):
        span = slice(b * BLOCK, (b + 1) * BLOCK)
        raw = stg[span, :]
        step = jnp.log1p(jnp.exp(dot_nt(raw, pick) + bias_row))
        run = base_cols - jnp.dot(
            lower, step * decay_row, precision=HIGHEST, preferred_element_type=F32
        )
        base_cols = run[BLOCK - 1 :, :]
        gap = run * LOG2E - jnp.log(step) * LOG2E
        for k in range(chunks):
            run_cols[k, span, :] = run[:, k * chunk_heads : (k + 1) * chunk_heads] * LOG2E
            gap_cols[k, span, :] = gap[:, k * chunk_heads : (k + 1) * chunk_heads]
        step = jnp.log1p(jnp.exp(dot_nt(pick, raw) + bias_col))
        run = base_rows - dot_nt(step * decay_col, lower, precision=HIGHEST)
        base_rows = run[:, BLOCK - 1 :]
        gap = run * LOG2E - jnp.log(step) * LOG2E
        for k in range(chunks):
            gap_rows[k, :, span] = gap[k * chunk_heads : (k + 1) * chunk_heads, :]
    spread = (
        lax.broadcasted_iota(jnp.int32, (heads, width), 1) // HEAD_DIM
        == lax.broadcasted_iota(jnp.int32, (heads, width), 0)
    ).astype(F32)
    skip_lanes[...] = jnp.dot(
        jnp.broadcast_to(skip_ref[...], (8, heads)),
        spread,
        precision=HIGHEST,
        preferred_element_type=F32,
    )

    def convolve(raw, state, weight, bias):
        conv_rows[8 - CONV_K + 1 : 8, :] = state.astype(F32)
        conv_rows[8:, :] = raw.astype(F32)
        total = jnp.broadcast_to(bias, (length, PAIR))
        for tap in range(CONV_K):
            start = 8 - CONV_K + 1 + tap
            total = total + weight[tap : tap + 1, :].astype(F32) * conv_rows[start : start + length, :]
        return silu(total).astype(BF16)

    arrive_from_all(bc_copy)
    for j in range(group_width // PAIR):
        cols = pl.ds(pl.multiple_of(group * group_width + j * PAIR, PAIR), PAIR)
        maps[:, j * PAIR : (j + 1) * PAIR] = convolve(
            bcg[:, j * PAIR : (j + 1) * PAIR],
            state_bc_ref[:, cols],
            weight_bc_ref[:, cols],
            bias_bc_ref[pl.ds(group * (group_width // PAIR) + j, 1), :],
        )
    for q in range(blocks):
        here = slice(q * BLOCK, (q + 1) * BLOCK)
        for s in range(q + 1):
            there = slice(s * BLOCK, (s + 1) * BLOCK)
            scores = dot_nt(maps[here, STATE:], maps[there, :STATE])
            masked_scores[here, there] = jnp.where(below, scores, 0.0) if s == q else scores
    tail_cols = tail_bc_ref.shape[1]
    offset = pl.multiple_of(me * tail_cols - group * group_width, tail_cols)
    tail_bc_ref[...] = bcg[length - 16 :, pl.ds(offset, tail_cols)][16 - CONV_K + 1 :, :]

    first_lanes = lax.broadcasted_iota(jnp.int32, (BLOCK, PAIR), 1) < HEAD_DIM
    first_rows = lax.broadcasted_iota(jnp.int32, (PAIR, 1), 0) < HEAD_DIM

    def one_chunk(k, carry):
        arrive_from_all(lambda i, peer, source: x_copy(i, k, peer, source))
        scan_copy(k).wait()
        for j in range(chunk // PAIR):
            cols = pl.ds(pl.multiple_of(k * chunk + j * PAIR, PAIR), PAIR)
            mixed = convolve(
                xg[:, cols],
                state_x_ref[:, cols],
                weight_x_ref[:, cols],
                bias_x_ref[pl.ds(k * (chunk // PAIR) + j, 1), :],
            )
            old = scan[cols, :]
            high = old.astype(BF16)
            low = (old - high.astype(F32)).astype(BF16)
            ends = [run_cols[k, length - 1 :, 2 * j + h : 2 * j + h + 1] for h in (0, 1)]
            gained = None
            for q in range(blocks):
                here = slice(q * BLOCK, (q + 1) * BLOCK)
                values = mixed[here, :].astype(F32)
                out = maps[here, STATE:]
                run = [
                    jnp.broadcast_to(run_cols[k, here, 2 * j + h : 2 * j + h + 1], (BLOCK, PAIR))
                    for h in (0, 1)
                ]
                total = (dot_nt(out, high) + dot_nt(out, low)) * jnp.where(
                    first_lanes, jnp.exp2(run[0]), jnp.exp2(run[1])
                )
                total = total + skip_lanes[0:1, cols] * values
                for s in range(q + 1):
                    there = slice(s * BLOCK, (s + 1) * BLOCK)
                    for h in (0, 1):
                        row = gap_rows[k, 2 * j + h : 2 * j + h + 1, there]
                        wide = jnp.concatenate([run[h]] * (BLOCK // PAIR), axis=1)
                        decayed = jnp.exp2(jnp.minimum(wide - row, 64.0))
                        weights = (masked_scores[here, there] * decayed).astype(BF16)
                        keep = first_lanes if h == 0 else jnp.logical_not(first_lanes)
                        seen = jnp.where(keep, mixed[there, :].astype(F32), 0.0).astype(BF16)
                        total = total + jnp.dot(weights, seen, preferred_element_type=F32)
                ysend[here, cols] = total.astype(BF16)
                tails = [
                    jnp.exp2(ends[h] - gap_cols[k, here, 2 * j + h : 2 * j + h + 1]) for h in (0, 1)
                ]
                tailed = (values * jnp.where(first_lanes, tails[0], tails[1])).astype(BF16)
                part = dot_tn(tailed, maps[here, :STATE])
                gained = part if gained is None else gained + part
            fade = jnp.where(first_rows, jnp.exp2(ends[0]), jnp.exp2(ends[1]))
            fout[cols, :] = fade * old + gained
        start_to_all(lambda i, peer, source: y_copy(i, k, peer, source))
        fout_copy(k).start()
        return carry

    lax.fori_loop(0, chunks, one_chunk, 0)
    tail_x_ref[...] = xg[length - 16 :, :][16 - CONV_K + 1 :, :]

    for copy in tail_copies:
        copy.start()

    members = max(1, n // GROUPS)
    spans = []
    norm_width = nout.shape[1] // GROUPS

    def arrive(i):
        for k in range(chunks):
            if i == 0:
                y_copy(0, k, me, me).wait()
            else:
                y_copy(i, k, partner(i), partner(i)).wait_recv()

    if members > 1:
        for i in range(n):
            arrive(i)
    for q in range(GROUPS):
        if members == 1:
            arrive(q)
            start = partner(q) * norm_width
        else:
            start = q * norm_width
        span = pl.ds(pl.multiple_of(start, norm_width), norm_width)
        values = yrecv[:, span].astype(F32)
        inverse = lax.rsqrt(jnp.mean(values * values, axis=1, keepdims=True) + EPSILON)
        first = start // PAIR
        for j in range(norm_width // PAIR):
            cols = pl.ds(pl.multiple_of(start + j * PAIR, PAIR), PAIR)
            scaled = yrecv[:, cols].astype(F32) * inverse
            nout[:, cols] = (scaled * norm_ref[pl.ds(first + j, 1), :]).astype(BF16)
        nout_copy(q, span).start()
        spans.append(span)

    for i in range(1, n):
        step_copy(i, partner(i), me).wait_send()
        bc_copy(i, partner(i), me).wait_send()
        for k in range(chunks):
            x_copy(i, k, partner(i), me).wait_send()
            y_copy(i, k, partner(i), me).wait_send()
    for k in range(chunks):
        fout_copy(k).wait()
    for q in range(GROUPS):
        nout_copy(q, spans[q]).wait()
    for copy in tail_copies:
        copy.wait()

def write_out(*refs):
    arrive, leave = [], []
    for i in range(4):
        source, target, stage = refs[i], refs[4 + i], refs[8 + i]
        size = source.shape[0] // SPLITS[i]
        for p in range(SPLITS[i]):
            span = pl.ds(p * size, size)
            sem = len(arrive)
            arrive.append(
                pltpu.make_async_copy(source.at[span, :], stage.at[span, :], refs[12].at[sem])
            )
            leave.append(
                pltpu.make_async_copy(stage.at[span, :], target.at[span, :], refs[13].at[sem])
            )
    for copy in arrive:
        copy.start()
    for first, second in zip(arrive, leave):
        first.wait()
        second.start()
    for copy in leave:
        copy.wait()


def local(
    inner_x,
    inner_bc,
    step_raw,
    conv_state_x,
    conv_state_bc,
    conv_weight_x,
    conv_bias_x,
    conv_weight_bc,
    conv_bias_bc,
    step_bias,
    decay_rate,
    skip_gain,
    norm_weight,
    scan_state,
):
    n = lax.axis_size("tensor")
    rows, inner = inner_x.shape
    heads = step_bias.shape[0]
    width = heads * HEAD_DIM
    length = n * rows
    chunk = min(CHUNK, width)
    chunks = width // chunk
    chunk_heads = chunk // HEAD_DIM
    group_width = 2 * STATE
    tail_cols = inner_bc.shape[1] // n
    dma = pltpu.SemaphoreType.DMA
    hbm = pl.BlockSpec(memory_space=pltpu.HBM)
    small = (
        conv_state_x,
        conv_state_bc,
        conv_weight_x,
        conv_bias_x.reshape(-1, PAIR),
        conv_weight_bc,
        conv_bias_bc.reshape(-1, PAIR),
        step_bias.reshape(1, -1),
        decay_rate.reshape(1, -1),
        skip_gain.reshape(1, -1),
        norm_weight.reshape(-1, PAIR),
    )
    out_shape = (
        jax.ShapeDtypeStruct((rows, inner), BF16),
        jax.ShapeDtypeStruct((width, STATE), F32),
        jax.ShapeDtypeStruct((CONV_K - 1, width), BF16),
        jax.ShapeDtypeStruct((CONV_K - 1, tail_cols), BF16),
    )
    outs = pl.pallas_call(
        functools.partial(kernel, n, chunk),
        out_shape=out_shape,
        in_specs=[hbm] * 14,
        out_specs=(hbm,) * 4,
        scratch_shapes=[pltpu.VMEM(a.shape, a.dtype) for a in small]
        + [
            pltpu.VMEM((length, width), BF16),
            pltpu.VMEM((length, group_width), BF16),
            pltpu.VMEM((length, step_raw.shape[1]), BF16),
            pltpu.VMEM((length, width), BF16),
            pltpu.VMEM((rows, inner), BF16),
            pltpu.VMEM((width, STATE), F32),
            pltpu.VMEM((width, STATE), F32),
            pltpu.VMEM((rows, inner), BF16),
            pltpu.VMEM(out_shape[2].shape, BF16),
            pltpu.VMEM(out_shape[3].shape, BF16),
            pltpu.VMEM((length + 8, PAIR), F32),
            pltpu.VMEM((length, group_width), BF16),
            pltpu.VMEM((length, length), F32),
            pltpu.VMEM((chunks, length, chunk_heads), F32),
            pltpu.VMEM((chunks, length, chunk_heads), F32),
            pltpu.VMEM((chunks, chunk_heads, length), F32),
            pltpu.VMEM((8, width), F32),
            pltpu.VMEM(small[3].shape, F32),
            pltpu.VMEM(small[5].shape, F32),
            pltpu.VMEM(small[9].shape, F32),
            dma((2, n)),
            dma((2, n)),
            dma((n, chunks)),
            dma((n, chunks)),
            dma((n, chunks)),
            dma((n, chunks)),
            dma((chunks,)),
            dma((len(small),)),
            dma((chunks,)),
            dma((GROUPS,)),
            dma((2,)),
        ],
        compiler_params=pltpu.CompilerParams(
            collective_id=0, has_side_effects=True, vmem_limit_bytes=VMEM_LIMIT
        ),
    )(
        inner_x,
        inner_bc,
        step_raw,
        *small,
        scan_state.reshape(width, STATE),
    )
    outs = pl.pallas_call(
        write_out,
        out_shape=out_shape,
        in_specs=[hbm] * 4,
        out_specs=(hbm,) * 4,
        scratch_shapes=[pltpu.VMEM(a.shape, a.dtype) for a in out_shape]
        + [dma((sum(SPLITS),)), dma((sum(SPLITS),))],
        compiler_params=pltpu.CompilerParams(vmem_limit_bytes=VMEM_LIMIT),
    )(*outs)
    normed, final_state, tail_x, tail_bc = outs
    return (normed, final_state.reshape(heads, HEAD_DIM, STATE), tail_x, tail_bc)


def solution(mesh):
    return jax.shard_map(
        local,
        mesh=mesh,
        in_specs=(
            P(("dp", "tensor"), None),
            P(("dp", "tensor"), None),
            P(("dp", "tensor"), None),
            P("dp", "tensor"),
            P("dp", None),
            P(None, "tensor"),
            P("tensor"),
            P(),
            P(),
            P("tensor"),
            P("tensor"),
            P("tensor"),
            P(),
            P(("dp", "tensor"), None, None),
        ),
        out_specs=(
            P(("dp", "tensor"), None),
            P(("dp", "tensor"), None, None),
            P("dp", "tensor"),
            P("dp", "tensor"),
        ),
        check_vma=False,
    )
```

```python
import functools
import math

import jax
import jax.numpy as jnp
from jax import lax
from jax.experimental import pallas as pl
from jax.experimental.pallas import tpu as pltpu
from jax.sharding import PartitionSpec as P

HEAD_DIM = 64
STATE = 256
GROUPS = 4
CONV_K = 4
EPSILON = 1e-05
LOG2E = math.log2(math.e)
CHUNK = 512
SPLITS = (4, 8, 1, 1)
VMEM_LIMIT = 60 * 1024 * 1024
PAIR = 2 * HEAD_DIM
BLOCK = 256
MESH = pl.DeviceIdType.MESH
F32 = jnp.float32
BF16 = jnp.bfloat16
HIGHEST = lax.Precision.HIGHEST


def dot_nt(a, b, precision=None):
    return lax.dot_general(
        a, b, (((1,), (1,)), ((), ())), precision=precision, preferred_element_type=F32
    )


def dot_tn(a, b):
    return lax.dot_general(a, b, (((0,), (0,)), ((), ())), preferred_element_type=F32)


def silu(total):
    half = 0.5 * total
    return half + half * jnp.tanh(half)


def column_of(row):
    width = row.shape[1]
    eye = lax.broadcasted_iota(jnp.int32, (width, width), 0) == lax.broadcasted_iota(
        jnp.int32, (width, width), 1
    )
    return jnp.sum(jnp.where(eye, jnp.broadcast_to(row, (width, width)), 0.0), axis=1, keepdims=True)


def kernel(
    n,
    chunk,
    x_ref,
    bc_ref,
    step_ref,
    *refs,
):
    small_in = refs[:10]
    scan_ref, normed_out, final_out, tail_x_out, tail_bc_out = refs[10:15]
    small = refs[15:25]
    (
        state_x_ref,
        state_bc_ref,
        weight_x_ref,
        bias_x_in,
        weight_bc_ref,
        bias_bc_in,
        step_bias_ref,
        decay_ref,
        skip_ref,
        norm_in,
    ) = small
    (
        xg,
        bcg,
        stg,
        ysend,
        scan,
        fout,
        tail_x_ref,
        tail_bc_ref,
        conv_rows,
        maps,
        masked_scores,
        run_cols,
        gap_cols,
        gap_rows,
        skip_lanes,
        bias_x_ref,
        bias_bc_ref,
        norm_ref,
        small_send,
        small_recv,
        x_send,
        x_recv,
        y_send,
        y_recv,
        scan_sem,
        local_sem,
        fout_sem,
        tail_sem,
    ) = refs[25:]
    me = lax.axis_index("tensor")
    rows = x_ref.shape[0]
    length = n * rows
    width = xg.shape[1]
    chunks = width // chunk
    chunk_heads = chunk // HEAD_DIM
    heads = width // HEAD_DIM
    group_width = 2 * STATE
    blocks = length // BLOCK
    group = me * GROUPS // n

    order = list(range(n // 2, n)) + list(range(1, n // 2)) + [0]

    def partner(i):
        other, bit = me, 1
        while bit <= i:
            if i & bit:
                other = other + bit - 2 * bit * ((me // bit) % 2)
            bit *= 2
        return other

    def row_span(device):
        return pl.ds(pl.multiple_of(device * rows, rows), rows)

    def chunk_span(base, k):
        return pl.ds(pl.multiple_of(base + k * chunk, chunk), chunk)

    def group_span(device):
        start = (device * GROUPS // n) * group_width
        return pl.ds(pl.multiple_of(start, group_width), group_width)

    def bc_copy(i, peer, source):
        src, dst = bc_ref.at[:, group_span(peer)], bcg.at[row_span(source), :]
        if i == 0:
            return pltpu.make_async_copy(src, dst, small_recv.at[0, 0])
        return pltpu.make_async_remote_copy(
            src, dst, small_send.at[0, i], small_recv.at[0, i], {"tensor": peer}, MESH
        )

    def step_copy(i, peer, source):
        src, dst = step_ref, stg.at[row_span(source), :]
        if i == 0:
            return pltpu.make_async_copy(src, dst, small_recv.at[1, 0])
        return pltpu.make_async_remote_copy(
            src, dst, small_send.at[1, i], small_recv.at[1, i], {"tensor": peer}, MESH
        )

    def x_copy(i, k, peer, source):
        src = x_ref.at[:, chunk_span(peer * width, k)]
        dst = xg.at[row_span(source), chunk_span(0, k)]
        if i == 0:
            return pltpu.make_async_copy(src, dst, x_recv.at[0, k])
        return pltpu.make_async_remote_copy(
            src, dst, x_send.at[i, k], x_recv.at[i, k], {"tensor": peer}, MESH
        )

    def y_copy(i, k, peer, source):
        src = ysend.at[row_span(peer), chunk_span(0, k)]
        dst = normed_out.at[:, chunk_span(source * width, k)]
        if i == 0:
            return pltpu.make_async_copy(src, dst, y_recv.at[0, k])
        return pltpu.make_async_remote_copy(
            src, dst, y_send.at[i, k], y_recv.at[i, k], {"tensor": peer}, MESH
        )

    def scan_copy(k):
        return pltpu.make_async_copy(
            scan_ref.at[chunk_span(0, k), :], scan.at[chunk_span(0, k), :], scan_sem.at[k]
        )

    def small_copy(i):
        return pltpu.make_async_copy(small_in[i], small[i], local_sem.at[i])

    def fout_copy(k):
        span = chunk_span(0, k)
        return pltpu.make_async_copy(fout.at[span, :], final_out.at[span, :], fout_sem.at[k])

    tail_copies = (
        pltpu.make_async_copy(tail_x_ref, tail_x_out, tail_sem.at[0]),
        pltpu.make_async_copy(tail_bc_ref, tail_bc_out, tail_sem.at[1]),
    )

    def start_to_all(copy):
        for i in order:
            copy(i, partner(i), me).start()

    def arrive_from_all(copy):
        for i in range(n):
            if i == 0:
                copy(0, me, me).wait()
            else:
                copy(i, partner(i), partner(i)).wait_recv()

    for i in range(len(small)):
        small_copy(i).start()
    barrier = pltpu.get_barrier_semaphore()
    for i in range(1, n):
        pl.semaphore_signal(barrier, inc=1, device_id={"tensor": partner(i)}, device_id_type=MESH)
    pl.semaphore_wait(barrier, n - 1)

    start_to_all(step_copy)
    start_to_all(bc_copy)
    for k in range(chunks):
        start_to_all(lambda i, peer, source: x_copy(i, k, peer, source))
    for k in range(chunks):
        scan_copy(k).start()

    for i in range(len(small)):
        small_copy(i).wait()
    bias_x_ref[...] = bias_x_in[...].astype(F32)
    bias_bc_ref[...] = bias_bc_in[...].astype(F32)
    norm_ref[...] = norm_in[...].astype(F32)

    arrive_from_all(step_copy)
    lanes_all = stg.shape[1]
    pick = (
        lax.broadcasted_iota(jnp.int32, (heads, lanes_all), 1)
        == lax.broadcasted_iota(jnp.int32, (heads, lanes_all), 0) + me * heads
    ).astype(BF16)
    bias_row, decay_row = step_bias_ref[...], decay_ref[...]
    bias_col, decay_col = column_of(bias_row), column_of(decay_row)
    below = (
        lax.broadcasted_iota(jnp.int32, (BLOCK, BLOCK), 0)
        >= lax.broadcasted_iota(jnp.int32, (BLOCK, BLOCK), 1)
    )
    lower = below.astype(F32)
    base_cols = jnp.zeros((1, heads), F32)
    base_rows = jnp.zeros((heads, 1), F32)
    for b in range(blocks):
        span = slice(b * BLOCK, (b + 1) * BLOCK)
        raw = stg[span, :]
        step = jnp.log1p(jnp.exp(dot_nt(raw, pick) + bias_row))
        run = base_cols - jnp.dot(
            lower, step * decay_row, precision=HIGHEST, preferred_element_type=F32
        )
        base_cols = run[BLOCK - 1 :, :]
        gap = run * LOG2E - jnp.log(step) * LOG2E
        for k in range(chunks):
            run_cols[k, span, :] = run[:, k * chunk_heads : (k + 1) * chunk_heads] * LOG2E
            gap_cols[k, span, :] = gap[:, k * chunk_heads : (k + 1) * chunk_heads]
        step = jnp.log1p(jnp.exp(dot_nt(pick, raw) + bias_col))
        run = base_rows - dot_nt(step * decay_col, lower, precision=HIGHEST)
        base_rows = run[:, BLOCK - 1 :]
        gap = run * LOG2E - jnp.log(step) * LOG2E
        for k in range(chunks):
            gap_rows[k, :, span] = gap[k * chunk_heads : (k + 1) * chunk_heads, :]
    spread = (
        lax.broadcasted_iota(jnp.int32, (heads, width), 1) // HEAD_DIM
        == lax.broadcasted_iota(jnp.int32, (heads, width), 0)
    ).astype(F32)
    skip_lanes[...] = jnp.dot(
        jnp.broadcast_to(skip_ref[...], (8, heads)),
        spread,
        precision=HIGHEST,
        preferred_element_type=F32,
    )

    def convolve(raw, state, weight, bias):
        conv_rows[8 - CONV_K + 1 : 8, :] = state.astype(F32)
        conv_rows[8:, :] = raw.astype(F32)
        total = jnp.broadcast_to(bias, (length, PAIR))
        for tap in range(CONV_K):
            start = 8 - CONV_K + 1 + tap
            total = total + weight[tap : tap + 1, :].astype(F32) * conv_rows[start : start + length, :]
        return silu(total).astype(BF16)

    arrive_from_all(bc_copy)
    for j in range(group_width // PAIR):
        cols = pl.ds(pl.multiple_of(group * group_width + j * PAIR, PAIR), PAIR)
        maps[:, j * PAIR : (j + 1) * PAIR] = convolve(
            bcg[:, j * PAIR : (j + 1) * PAIR],
            state_bc_ref[:, cols],
            weight_bc_ref[:, cols],
            bias_bc_ref[pl.ds(group * (group_width // PAIR) + j, 1), :],
        )
    for q in range(blocks):
        here = slice(q * BLOCK, (q + 1) * BLOCK)
        for s in range(q + 1):
            there = slice(s * BLOCK, (s + 1) * BLOCK)
            scores = dot_nt(maps[here, STATE:], maps[there, :STATE])
            masked_scores[here, there] = jnp.where(below, scores, 0.0) if s == q else scores
    tail_cols = tail_bc_ref.shape[1]
    offset = pl.multiple_of(me * tail_cols - group * group_width, tail_cols)
    tail_bc_ref[...] = bcg[length - 16 :, pl.ds(offset, tail_cols)][16 - CONV_K + 1 :, :]

    first_lanes = lax.broadcasted_iota(jnp.int32, (BLOCK, PAIR), 1) < HEAD_DIM
    first_rows = lax.broadcasted_iota(jnp.int32, (PAIR, 1), 0) < HEAD_DIM

    def one_chunk(k, carry):
        arrive_from_all(lambda i, peer, source: x_copy(i, k, peer, source))
        scan_copy(k).wait()
        for j in range(chunk // PAIR):
            cols = pl.ds(pl.multiple_of(k * chunk + j * PAIR, PAIR), PAIR)
            mixed = convolve(
                xg[:, cols],
                state_x_ref[:, cols],
                weight_x_ref[:, cols],
                bias_x_ref[pl.ds(k * (chunk // PAIR) + j, 1), :],
            )
            old = scan[cols, :]
            high = old.astype(BF16)
            low = (old - high.astype(F32)).astype(BF16)
            ends = [run_cols[k, length - 1 :, 2 * j + h : 2 * j + h + 1] for h in (0, 1)]
            gained = None
            for q in range(blocks):
                here = slice(q * BLOCK, (q + 1) * BLOCK)
                values = mixed[here, :].astype(F32)
                out = maps[here, STATE:]
                run = [
                    jnp.broadcast_to(run_cols[k, here, 2 * j + h : 2 * j + h + 1], (BLOCK, PAIR))
                    for h in (0, 1)
                ]
                total = (dot_nt(out, high) + dot_nt(out, low)) * jnp.where(
                    first_lanes, jnp.exp2(run[0]), jnp.exp2(run[1])
                )
                total = total + skip_lanes[0:1, cols] * values
                for s in range(q + 1):
                    there = slice(s * BLOCK, (s + 1) * BLOCK)
                    for h in (0, 1):
                        row = gap_rows[k, 2 * j + h : 2 * j + h + 1, there]
                        wide = jnp.concatenate([run[h]] * (BLOCK // PAIR), axis=1)
                        decayed = jnp.exp2(jnp.minimum(wide - row, 64.0))
                        weights = (masked_scores[here, there] * decayed).astype(BF16)
                        keep = first_lanes if h == 0 else jnp.logical_not(first_lanes)
                        seen = jnp.where(keep, mixed[there, :].astype(F32), 0.0).astype(BF16)
                        total = total + jnp.dot(weights, seen, preferred_element_type=F32)
                ysend[here, cols] = total.astype(BF16)
                tails = [
                    jnp.exp2(ends[h] - gap_cols[k, here, 2 * j + h : 2 * j + h + 1]) for h in (0, 1)
                ]
                tailed = (values * jnp.where(first_lanes, tails[0], tails[1])).astype(BF16)
                part = dot_tn(tailed, maps[here, :STATE])
                gained = part if gained is None else gained + part
            fade = jnp.where(first_rows, jnp.exp2(ends[0]), jnp.exp2(ends[1]))
            fout[cols, :] = fade * old + gained
        start_to_all(lambda i, peer, source: y_copy(i, k, peer, source))
        fout_copy(k).start()
        return carry

    lax.fori_loop(0, chunks, one_chunk, 0)
    tail_x_ref[...] = xg[length - 16 :, :][16 - CONV_K + 1 :, :]

    for copy in tail_copies:
        copy.start()

    def arrive(i):
        for k in range(chunks):
            if i == 0:
                y_copy(0, k, me, me).wait()
            else:
                y_copy(i, k, partner(i), partner(i)).wait_recv()

    for i in range(n):
        arrive(i)

    for i in range(1, n):
        step_copy(i, partner(i), me).wait_send()
        bc_copy(i, partner(i), me).wait_send()
        for k in range(chunks):
            x_copy(i, k, partner(i), me).wait_send()
            y_copy(i, k, partner(i), me).wait_send()
    for k in range(chunks):
        fout_copy(k).wait()
    for copy in tail_copies:
        copy.wait()

def write_out(*refs):
    norm_in, norm_ref, norm_sem = refs[4], refs[15], refs[16]
    norm_copy = pltpu.make_async_copy(norm_in, norm_ref, norm_sem)
    norm_copy.start()
    arrive, leave = [], []
    for i in range(4):
        source, target, stage = refs[i], refs[5 + i], refs[9 + i]
        size = source.shape[0] // SPLITS[i]
        for p in range(SPLITS[i]):
            span = pl.ds(p * size, size)
            sem = len(arrive)
            arrive.append(
                pltpu.make_async_copy(source.at[span, :], stage.at[span, :], refs[13].at[sem])
            )
            leave.append(
                pltpu.make_async_copy(stage.at[span, :], target.at[span, :], refs[14].at[sem])
            )
    for copy in arrive:
        copy.start()
    norm_copy.wait()
    gains = norm_ref[...].astype(F32)
    stage = refs[9]
    size = stage.shape[0] // SPLITS[0]
    norm_width = stage.shape[1] // GROUPS
    for p in range(SPLITS[0]):
        span = slice(p * size, (p + 1) * size)
        arrive[p].wait()
        for q in range(GROUPS):
            values = stage[span, q * norm_width : (q + 1) * norm_width].astype(F32)
            inverse = lax.rsqrt(jnp.mean(values * values, axis=1, keepdims=True) + EPSILON)
            for j in range(q * norm_width // PAIR, (q + 1) * norm_width // PAIR):
                cols = slice(j * PAIR, (j + 1) * PAIR)
                scaled = stage[span, cols].astype(F32) * inverse
                stage[span, cols] = (scaled * gains[j : j + 1, :]).astype(BF16)
        leave[p].start()
        for k in range(SPLITS[0] + 2 * p, SPLITS[0] + 2 * p + 2):
            arrive[k].wait()
            leave[k].start()
    for k in range(3 * SPLITS[0], len(arrive)):
        arrive[k].wait()
        leave[k].start()
    for copy in leave:
        copy.wait()


def local(
    inner_x,
    inner_bc,
    step_raw,
    conv_state_x,
    conv_state_bc,
    conv_weight_x,
    conv_bias_x,
    conv_weight_bc,
    conv_bias_bc,
    step_bias,
    decay_rate,
    skip_gain,
    norm_weight,
    scan_state,
):
    n = lax.axis_size("tensor")
    rows, inner = inner_x.shape
    heads = step_bias.shape[0]
    width = heads * HEAD_DIM
    length = n * rows
    chunk = min(CHUNK, width)
    chunks = width // chunk
    chunk_heads = chunk // HEAD_DIM
    group_width = 2 * STATE
    tail_cols = inner_bc.shape[1] // n
    dma = pltpu.SemaphoreType.DMA
    hbm = pl.BlockSpec(memory_space=pltpu.HBM)
    small = (
        conv_state_x,
        conv_state_bc,
        conv_weight_x,
        conv_bias_x.reshape(-1, PAIR),
        conv_weight_bc,
        conv_bias_bc.reshape(-1, PAIR),
        step_bias.reshape(1, -1),
        decay_rate.reshape(1, -1),
        skip_gain.reshape(1, -1),
        norm_weight.reshape(-1, PAIR),
    )
    out_shape = (
        jax.ShapeDtypeStruct((rows, inner), BF16),
        jax.ShapeDtypeStruct((width, STATE), F32),
        jax.ShapeDtypeStruct((CONV_K - 1, width), BF16),
        jax.ShapeDtypeStruct((CONV_K - 1, tail_cols), BF16),
    )
    outs = pl.pallas_call(
        functools.partial(kernel, n, chunk),
        out_shape=out_shape,
        in_specs=[hbm] * 14,
        out_specs=(hbm,) * 4,
        scratch_shapes=[pltpu.VMEM(a.shape, a.dtype) for a in small]
        + [
            pltpu.VMEM((length, width), BF16),
            pltpu.VMEM((length, group_width), BF16),
            pltpu.VMEM((length, step_raw.shape[1]), BF16),
            pltpu.VMEM((length, width), BF16),
            pltpu.VMEM((width, STATE), F32),
            pltpu.VMEM((width, STATE), F32),
            pltpu.VMEM(out_shape[2].shape, BF16),
            pltpu.VMEM(out_shape[3].shape, BF16),
            pltpu.VMEM((length + 8, PAIR), F32),
            pltpu.VMEM((length, group_width), BF16),
            pltpu.VMEM((length, length), F32),
            pltpu.VMEM((chunks, length, chunk_heads), F32),
            pltpu.VMEM((chunks, length, chunk_heads), F32),
            pltpu.VMEM((chunks, chunk_heads, length), F32),
            pltpu.VMEM((8, width), F32),
            pltpu.VMEM(small[3].shape, F32),
            pltpu.VMEM(small[5].shape, F32),
            pltpu.VMEM(small[9].shape, F32),
            dma((2, n)),
            dma((2, n)),
            dma((n, chunks)),
            dma((n, chunks)),
            dma((n, chunks)),
            dma((n, chunks)),
            dma((chunks,)),
            dma((len(small),)),
            dma((chunks,)),
            dma((2,)),
        ],
        compiler_params=pltpu.CompilerParams(
            collective_id=0, has_side_effects=True, vmem_limit_bytes=VMEM_LIMIT
        ),
    )(
        inner_x,
        inner_bc,
        step_raw,
        *small,
        scan_state.reshape(width, STATE),
    )
    outs = pl.pallas_call(
        write_out,
        out_shape=out_shape,
        in_specs=[hbm] * 5,
        out_specs=(hbm,) * 4,
        scratch_shapes=[pltpu.VMEM(a.shape, a.dtype) for a in out_shape]
        + [dma((sum(SPLITS),)), dma((sum(SPLITS),)), pltpu.VMEM(small[9].shape, BF16), dma],
        compiler_params=pltpu.CompilerParams(vmem_limit_bytes=VMEM_LIMIT),
    )(*outs, small[9])
    normed, final_state, tail_x, tail_bc = outs
    return (normed, final_state.reshape(heads, HEAD_DIM, STATE), tail_x, tail_bc)


def solution(mesh):
    return jax.shard_map(
        local,
        mesh=mesh,
        in_specs=(
            P(("dp", "tensor"), None),
            P(("dp", "tensor"), None),
            P(("dp", "tensor"), None),
            P("dp", "tensor"),
            P("dp", None),
            P(None, "tensor"),
            P("tensor"),
            P(),
            P(),
            P("tensor"),
            P("tensor"),
            P("tensor"),
            P(),
            P(("dp", "tensor"), None, None),
        ),
        out_specs=(
            P(("dp", "tensor"), None),
            P(("dp", "tensor"), None, None),
            P("dp", "tensor"),
            P("dp", "tensor"),
        ),
        check_vma=False,
    )
```
